32 devices in a mesh: groups: 2 (over x), cells: 16 (over z, y, core).
Axes of the slice: x: 2, y: 2, z: 4, core: 2. Of those that a mesh axis runs over, the one named last changes fastest.
Arguments:
- probes: float32 [8, 16, 128, 512], P('groups', None, 'cells'), parts along dimension 0, may hold values from -6 to 6
- wind_field: float32 [3, 16, 128, 512], P(None, None, 'cells'), may hold values from -1 to 1
- prior_scale: float32 [16, 128, 512], P(None, 'cells'), may hold values from 0.5 to 3
- eigen_basis: float32 [128, 512, 128], P('cells'), may hold values from -0.0234375 to 0.0234375
- eigen_values: float32 [128], replicated, may hold values from 0.1 to 100
- kernel_rows: float32 [512, 512], P(('groups', 'cells')), parts along dimension 0, may hold values from 0.2 to 1
- obs_weight: float32 [512, 32], P(('groups', 'cells')), parts along dimension 0, may hold values from 0.3 to 3
- tile_column: int32 [512, 32], P(('groups', 'cells')), parts along dimension 0, may hold values from -1 to 4095, as said below
Outputs:
- hessian_probes: float32 [8, 16, 128, 512], P('groups', None, 'cells'), parts along dimension 0
- misfit: float32 [512, 128], P(('groups', 'cells')), parts along dimension 0
- coeffs: float32 [8, 128], P('groups'), parts along dimension 0
The draws below stay inside these ranges and needn't reach their ends.
There are 2 independent parts, one for each index of `groups`. The reference program is written for one: setup_inputs(seed, part) draws one part's arguments, and reference() takes and returns one part's arrays. A program takes and returns all parts, laid end to end along the dimension named above; an argument that names none is the same for every part. Nothing has to cross between parts.
Inputs may be any that keep to these rules, and one draw needn't show every extreme that they name: `tile_column`: -1 marks an empty slot; the live slots of a row come first; in every draw some tiles receive 32 live slots from every tile.
All inputs are finite; a program needn't handle non-finite values.
Results may differ from the reference program's by a relative error of at most 0.00013.
Values sent between devices are 32-bit elements; how exact they have to be, the bound alone decides.
A program may use at most 128 MiB of HBM per device.

```python
import math
import jax
import jax.numpy as jnp
from jax import lax

K = 4
LEV = 16
STEPS = 4
CLON = 8
LAT = 512
CAP = 32
RANK = 128
NTILES = 16
NLON = 128
PAIRS = 256


def draw_tile_column(key, part):
    key = jax.random.fold_in(key, 7)
    key_counts, key_dense, key_cols = jax.random.split(key, 3)
    counts = jax.random.randint(key_counts, (NTILES, NTILES), CAP // 2, CAP + 1)
    dense_tiles = jax.random.randint(key_dense, (3,), 0, NTILES)
    is_dense = jnp.any(jnp.arange(NTILES)[:, None] == dense_tiles[None, :], axis=1)
    counts = jnp.where(is_dense[:, None], CAP, counts)
    columns = jax.random.randint(key_cols, (NTILES, NTILES, CAP), 0, CLON * LAT)
    live = jnp.arange(CAP)[None, None, :] < counts[:, :, None]
    return jnp.where(live, columns, -1).reshape(NTILES * NTILES, CAP).astype(jnp.int32)


def block_levels(rng, dims, cuts, low, top_value):
    def one(axis_at, shards_of):
        steps = jax.random.uniform(jax.random.fold_in(jax.random.fold_in(rng, 6), axis_at), (shards_of,), jnp.float32, low / len(cuts), top_value / len(cuts))
        return jnp.repeat(jnp.exp(steps), dims[axis_at] // shards_of).reshape((-1,) + (1,) * (len(dims) - axis_at - 1))

    gain = one(*cuts[0])
    for cut in cuts[1:]:
        gain = gain * one(*cut)
    return gain


def noise(rng, extent, spread, limit, pieces=(), kind=jnp.bfloat16):
    values = spread * jax.random.normal(rng, extent, jnp.float32)
    if pieces:
        values = values * block_levels(rng, extent, pieces, -0.22, 0.18)
    return jnp.clip(values, -limit, limit).astype(kind)


def setup_inputs(seed: int = 0, part: int = 0) -> dict:
    key_of = jax.random.split(jax.random.key(seed), 9)
    part_splits = jax.random.split(jax.random.fold_in(key_of[8], part), 9)
    probes = noise(part_splits[0], (K, LEV, NLON, LAT), 1.0, 6.0, ((2, 16),), jnp.float32)
    wind_field = jnp.clip(jax.random.uniform(key_of[1], (3, LEV, NLON, LAT), jnp.float32, -1.0, 1.0) * block_levels(key_of[1], (3, LEV, NLON, LAT), ((2, 16),), -0.4, 0.0), -1.0, 1.0)
    prior_scale = jnp.clip(jnp.exp(math.log(3.0) - 1.7917595 * jax.random.uniform(key_of[2], (LEV, NLON, LAT), jnp.float32) ** block_levels(key_of[2], (LEV, NLON, LAT), ((1, 16),), -0.2, 0.2)), 0.5, 3.0)
    eigen_basis = noise(key_of[3], (NLON, LAT, RANK), (NLON * LAT) ** -0.5, 0.0234375, ((0, 16),), jnp.float32)
    eigen_values = jnp.clip(jnp.exp(jax.random.uniform(key_of[4], (RANK,), jnp.float32, math.log(0.1), math.log(100.0))), 0.1, 100.0)
    kernel_rows = jnp.clip(0.2 + 0.8 * jax.random.uniform(part_splits[5], (PAIRS, LEV * CAP), jnp.float32) ** block_levels(part_splits[5], (PAIRS, LEV * CAP), ((0, 16),), -0.2, 0.2), 0.2, 1.0)
    obs_weight = jnp.clip(jnp.exp(math.log(3.0) - 2.3025851 * jax.random.uniform(part_splits[6], (PAIRS, CAP), jnp.float32) ** block_levels(part_splits[6], (PAIRS, CAP), ((0, 16),), -0.2, 0.2)), 0.3, 3.0)
    tile_column = draw_tile_column(jax.random.fold_in(jax.random.fold_in(key_of[8], part), 71), part)
    return {"probes": probes, "wind_field": wind_field, "prior_scale": prior_scale, "eigen_basis": eigen_basis, "eigen_values": eigen_values, "kernel_rows": kernel_rows, "obs_weight": obs_weight, "tile_column": tile_column}


def courants(wind_field):
    return (0.3 * wind_field[0], 0.15 * wind_field[1], 0.025 * (1.0 + wind_field[2]))

def vertical_mixing(center, mixing):
    upward = mixing[1:] * (center[:, :-1] - center[:, 1:])
    nothing = jnp.zeros_like(upward[:, :1])
    return jnp.concatenate([nothing, upward], axis=1) - jnp.concatenate([upward, nothing], axis=1)

def forward_step(tracer, wind_field):
    east_rate, north_rate, mixing = courants(wind_field)
    east_pos = jnp.maximum(east_rate, 0.0)
    east_neg = jnp.minimum(east_rate, 0.0)
    west_flux = east_pos[:, 1:] * tracer[:, :, :-1] + east_neg[:, 1:] * tracer[:, :, 1:]
    center = tracer[:, :, 1:-1]
    result = center - (west_flux[:, :, 1:] - west_flux[:, :, :-1])
    north_pos = jnp.maximum(north_rate[:, 1:-1], 0.0)
    north_neg = jnp.minimum(north_rate[:, 1:-1], 0.0)
    south_flux = north_pos[..., 1:] * center[..., :-1] + north_neg[..., 1:] * center[..., 1:]
    nothing = jnp.zeros_like(south_flux[..., :1])
    all_faces = jnp.concatenate([nothing, south_flux, nothing], axis=-1)
    result = result - (all_faces[..., 1:] - all_faces[..., :-1])
    return result + vertical_mixing(center, mixing[:, 1:-1])

def extend(array):
    return jnp.concatenate([array[:, :, -1:], array, array[:, :, :1]], axis=2)

def reference(probes, wind_field, prior_scale, eigen_basis, eigen_values, kernel_rows, obs_weight, tile_column):
    wind_ext = extend(wind_field)

    def transport(tracer):
        for section_index in range(STEPS):
            tracer = forward_step(extend(tracer), wind_ext)
        return tracer
    start = prior_scale[None] * probes
    final_state, pullback = jax.vjp(transport, start)
    cells_tile = CLON * LAT
    tiled = final_state.reshape(K, LEV, NTILES, cells_tile)
    column_list = tile_column.reshape(NTILES, NTILES * CAP)
    present = column_list >= 0
    present_f = present.astype(jnp.float32)
    safe_column = jnp.maximum(column_list, 0).astype(jnp.int32)
    index_full = jnp.broadcast_to(safe_column[None, None], (K, LEV, NTILES, NTILES * CAP))
    sampled = jnp.take_along_axis(tiled, index_full, axis=3)
    kernel_slots = kernel_rows.reshape(NTILES, NTILES, LEV, CAP).transpose(2, 1, 0, 3).reshape(LEV, NTILES, NTILES * CAP)
    modeled = lax.optimization_barrier(jnp.sum(kernel_slots[None] * sampled, axis=1)) * present_f
    weight_owner = obs_weight.reshape(NTILES, NTILES, CAP).transpose(1, 0, 2).reshape(NTILES, NTILES * CAP)
    weighted = modeled * weight_owner[None]
    misfit = weighted.reshape(K, NTILES, NTILES, CAP).transpose(2, 1, 0, 3).reshape(PAIRS, K * CAP)
    contrib = kernel_slots[None] * weighted[:, None] * present_f
    stacked = contrib.transpose(2, 3, 0, 1).reshape(NTILES * NTILES * CAP, K, LEV)
    tile_ids = jnp.arange(NTILES, dtype=jnp.int32)[:, None] * cells_tile
    segment_ids = jnp.where(present, tile_ids + column_list.astype(jnp.int32), NTILES * cells_tile).reshape(-1).astype(jnp.int32)
    summed = jax.ops.segment_sum(stacked, segment_ids, num_segments=NTILES * cells_tile + 1)[:-1]
    injected = summed.reshape(NTILES, CLON, LAT, K, LEV).transpose(3, 4, 0, 1, 2).reshape(K, LEV, NLON, LAT)
    pulled, = pullback(injected)
    hessian_probes = probes + prior_scale[None] * pulled
    projection = jnp.einsum('kxy,xyr->kr', hessian_probes[:, 0], eigen_basis, precision=lax.Precision.HIGHEST)
    coeffs = eigen_values / (1.0 + eigen_values) * projection
    return (hessian_probes, misfit, coeffs)
```

```python
import functools

import jax
import jax.numpy as jnp
from jax import lax
from jax.experimental import pallas as pl
from jax.experimental.pallas import tpu as pltpu
from jax.sharding import PartitionSpec as P

MESH = pl.DeviceIdType.MESH
HIGHEST = lax.Precision.HIGHEST
LEV = 16
STEPS = 4
CAP = 32
LANES = 128
HALO = STEPS


def split_bf16(value):
    high = value.astype(jnp.bfloat16)
    low = (value - high.astype(jnp.float32)).astype(jnp.bfloat16)
    return high, low


def kernel(
    probes, wind, prior, basis, eigen_values, kernel_rows, obs_weight, tile_column,
    hess_out, misfit_out, coeffs_out,
    probes_v, wind_v, prior_v, basis_v, basis_split, hess_v,
    fwd, adj, east, north_mix, row_send, row_recv, rows_2d, slots, weighted, one_hot, sampled,
    mis_2d, mis_send, mis_recv, proj, proj_recv,
    load_sem, col_send, col_recv, row_ssem, row_rsem, slot_ssem, slot_rsem, wt_ssem, wt_rsem,
    mis_ssem, mis_rsem, proj_ssem, proj_rsem,
):
    group = lax.axis_index("groups")
    me = lax.axis_index("cells")
    n = lax.axis_size("cells")
    east_nbr = lax.rem(me + 1, n)
    west_nbr = lax.rem(me + n - 1, n)
    lat = probes.shape[1]
    lon = fwd.shape[1] - 2 * HALO
    probe_count = fwd.shape[2] // LEV
    rows = probe_count * LEV
    total = n * CAP
    per_probe = LEV * lon

    barrier = pltpu.get_barrier_semaphore()

    def greet(i, carry):
        pl.semaphore_signal(
            barrier, inc=1, device_id=(group, lax.rem(me + i, n)), device_id_type=MESH
        )
        return carry

    lax.fori_loop(1, n, greet, 0)

    def tile_loads(source, target, at):
        return [
            pltpu.make_async_copy(
                source.at[:, pl.ds(t * LANES, LANES)], target.at[t], load_sem.at[at, t]
            )
            for t in range(lat // LANES)
        ]

    loads = [
        tile_loads(prior, prior_v, 0),
        tile_loads(probes, probes_v, 1),
        tile_loads(wind, wind_v, 2),
        [pltpu.make_async_copy(basis, basis_v, load_sem.at[3, 0])],
    ]
    for load in loads:
        for piece in load:
            piece.start()

    def wait_loads(at):
        for piece in loads[at]:
            piece.wait()

    def column(ref, base, i):
        return jnp.concatenate(
            [ref[t, pl.ds(base + i, LEV, stride=lon), :] for t in range(lat // LANES)], axis=1
        )

    def stage_row(i, carry):
        row_send[i, :, 0 : LEV * CAP] = kernel_rows[pl.ds(i, 1), :]
        row_send[i, :, LEV * CAP : LEV * CAP + CAP] = obs_weight[pl.ds(i, 1), :]
        row_send[i, :, LEV * CAP + CAP :] = jnp.zeros((1, LANES - CAP), jnp.float32)
        return carry

    lax.fori_loop(0, n, stage_row, 0)

    wait_loads(0)
    wait_loads(1)

    def start_col(i):
        scale = column(prior_v, 0, i)
        for k in range(probe_count):
            fwd[0, HALO + i, k * LEV : (k + 1) * LEV, :] = (
                scale * column(probes_v, k * per_probe, i)
            )

    def wind_col(i):
        level = lax.broadcasted_iota(jnp.int32, (LEV, lat), 0)
        row = lax.broadcasted_iota(jnp.int32, (LEV, lat), 1)
        east[HALO + i] = 0.3 * column(wind_v, 0, i)
        north_mix[HALO + i, 0] = jnp.where(
            row == 0, 0.0, 0.15 * column(wind_v, per_probe, i)
        )
        north_mix[HALO + i, 1] = jnp.where(
            level == 0, 0.0, 0.025 * (1.0 + column(wind_v, 2 * per_probe, i))
        )

    edges = []
    for d in range(HALO):
        edges += [lon - 1 - d, d]
    for i in edges:
        start_col(i)
    wait_loads(2)
    for i in edges:
        wind_col(i)

    pl.semaphore_wait(barrier, n - 1)

    def row_copy(target, source_id):
        return pltpu.make_async_remote_copy(
            src_ref=row_send.at[target], dst_ref=row_recv.at[source_id],
            send_sem=row_ssem.at[target], recv_sem=row_rsem.at[source_id],
            device_id=(group, target), device_id_type=MESH,
        )

    def send_row(i, carry):
        row_copy(lax.rem(me + i, n), me).start()
        return carry

    lax.fori_loop(1, n, send_row, 0)

    arrays = (fwd.at[0], east, north_mix)

    def column_copy(kind, side, d):
        if side == 0:
            source, target, device = HALO + lon - 1 - d, HALO - 1 - d, east_nbr
        else:
            source, target, device = HALO + d, HALO + lon + d, west_nbr
        return pltpu.make_async_remote_copy(
            src_ref=arrays[kind].at[source], dst_ref=arrays[kind].at[target],
            send_sem=col_send.at[kind, side, d], recv_sem=col_recv.at[kind, side, d],
            device_id=(group, device), device_id_type=MESH,
        )

    sends = []
    for d in range(HALO):
        for kind in range(3):
            if kind == 2 and d == HALO - 1:
                continue
            for side in range(2):
                if kind == 1 and d == HALO - 1 and side == 0:
                    continue
                sends.append(column_copy(kind, side, d))
                sends[-1].start()

    def forward_col(s, e):
        east_here = east[e]
        east_next = east[e + 1]
        north = north_mix[e, 0]
        mixing = north_mix[e, 1]
        for k in range(probe_count):
            part = pl.ds(k * LEV, LEV)
            center = fwd[s, e, part, :]
            flux = east_here * jnp.where(east_here > 0.0, fwd[s, e - 1, part, :], center)
            flux_next = east_next * jnp.where(east_next > 0.0, center, fwd[s, e + 1, part, :])
            south = north * jnp.where(north > 0.0, pltpu.roll(center, 1, 1), center)
            up = mixing * (pltpu.roll(center, 1, 0) - center)
            fwd[s + 1, e, part, :] = (
                center - (flux_next - flux) - (pltpu.roll(south, lat - 1, 1) - south)
                + (up - pltpu.roll(up, LEV - 1, 0))
            )

    def backward_col(s, e):
        east_neg = jnp.minimum(east[e], 0.0)
        east_pos = jnp.maximum(east[e + 1], 0.0)
        north = north_mix[e, 0]
        mixing = north_mix[e, 1]
        north_pos = jnp.maximum(north, 0.0)
        north_neg = jnp.minimum(north, 0.0)
        for k in range(probe_count):
            part = pl.ds(k * LEV, LEV)
            center = adj[s, e, part, :]
            diff = center - pltpu.roll(center, 1, 1)
            up = mixing * (pltpu.roll(center, 1, 0) - center)
            adj[s + 1, e, part, :] = (
                center
                + east_pos * (adj[s, e + 1, part, :] - center)
                + east_neg * (center - adj[s, e - 1, part, :])
                + pltpu.roll(north_pos * diff, lat - 1, 1) + north_neg * diff
                + (up - pltpu.roll(up, LEV - 1, 0))
            )

    def interior(col):
        for s in range(STEPS - 1):
            def body(i, carry, s=s):
                col(s, HALO + i)
                return carry

            lax.fori_loop(s + 1, lon - 1 - s, body, 0)

    def diagonal(col, d):
        def body(s, carry):
            col(s, HALO - d + s)
            col(s, HALO + lon - 1 + d - s)
            return carry

        lax.fori_loop(0, STEPS, body, 0)

    for i in range(HALO, lon - HALO):
        start_col(i)
        wind_col(i)
    interior(forward_col)

    row_recv[me] = row_send[me]

    def row_arrival(i, carry):
        source = lax.rem(me + i, n)
        row_copy(source, source).wait_recv()
        return carry

    lax.fori_loop(1, n, row_arrival, 0)

    def flatten_row(i, carry):
        rows_2d[pl.ds(i, 1), :] = row_recv[i]
        return carry

    lax.fori_loop(0, n, flatten_row, 0)

    slot_id = lax.broadcasted_iota(jnp.int32, (n, total), 1)
    holder = lax.broadcasted_iota(jnp.int32, (n, total), 0)
    held = (slot_id >> 5) == holder

    def spread(block, offset):
        lane = lax.broadcasted_iota(jnp.int32, (block.shape[1], total), 0)
        slot = lax.broadcasted_iota(jnp.int32, (block.shape[1], total), 1)
        pick = jnp.where(lane == (slot & (CAP - 1)) + offset, 1.0, 0.0)
        wide = jnp.dot(block, pick, precision=HIGHEST, preferred_element_type=jnp.float32)
        return jnp.sum(jnp.where(held, wide, 0.0), axis=0, keepdims=True)

    for level in range(LEV):
        tile = level * CAP // LANES
        slots[0, level : level + 1, :] = spread(
            rows_2d[:, tile * LANES : (tile + 1) * LANES], level * CAP % LANES
        )
    weight_row = spread(rows_2d[:, LEV * CAP :], 0)
    slots[0, LEV : LEV + 1, :] = spread(tile_column[...].astype(jnp.float32), 0)
    slots[0, LEV + 1 :, :] = jnp.zeros((slots.shape[1] - LEV - 1, total), jnp.float32)

    def slot_copy(side):
        return pltpu.make_async_remote_copy(
            src_ref=slots.at[0], dst_ref=slots.at[1 + side],
            send_sem=slot_ssem.at[side], recv_sem=slot_rsem.at[side],
            device_id=(group, (east_nbr, west_nbr)[side]), device_id_type=MESH,
        )

    for side in range(2):
        sends.append(slot_copy(side))
        sends[-1].start()

    def columns_of(which):
        column = slots[which, LEV : LEV + 1, :].astype(jnp.int32)
        return column, column >> (lat.bit_length() - 1)

    def make_one_hot(which):
        column, _ = columns_of(which)
        row = jnp.where(column < 0, -1, column & (lat - 1))
        place = lax.broadcasted_iota(jnp.int32, (lat, total), 0)
        one_hot[which] = jnp.where(place == row, 1.0, 0.0).astype(jnp.bfloat16)

    make_one_hot(0)
    sampled[...] = jnp.zeros_like(sampled)
    wait_loads(3)

    def split_basis(i, carry):
        high, low = split_bf16(basis_v[i])
        basis_split[i, :, 0:LANES] = high
        basis_split[i, :, LANES:] = low
        return carry

    lax.fori_loop(0, lon, split_basis, 0)

    def forward_diagonal(d, carry):
        for side in range(2):
            pltpu.make_async_remote_copy(
                src_ref=fwd.at[0, 0], dst_ref=fwd.at[0, 0],
                send_sem=col_send.at[0, side, d - 1], recv_sem=col_recv.at[0, side, d - 1],
                device_id=(group, east_nbr), device_id_type=MESH,
            ).wait_recv()

        def wait_wind(kind, side, at):
            pltpu.make_async_remote_copy(
                src_ref=arrays[kind].at[0], dst_ref=arrays[kind].at[0],
                send_sem=col_send.at[kind, side, at], recv_sem=col_recv.at[kind, side, at],
                device_id=(group, east_nbr), device_id_type=MESH,
            ).wait_recv()

        wait_wind(1, 1, d - 1)

        @pl.when(d > 1)
        def _():
            wait_wind(1, 0, d - 2)
            wait_wind(2, 0, d - 2)
            wait_wind(2, 1, d - 2)

        diagonal(forward_col, d - 1)
        pair = (HALO - d, lon - 1 - HALO + d)
        parts = []
        for i in pair:
            parts += split_bf16(fwd[STEPS, HALO + i])
        found = jnp.dot(
            jnp.concatenate(parts, axis=0), one_hot[0], preferred_element_type=jnp.float32
        )
        _, lon_row = columns_of(0)
        picked = sampled[...]
        for at, i in enumerate(pair):
            base = 2 * rows * at
            both = found[base : base + rows] + found[base + rows : base + 2 * rows]
            picked = picked + jnp.where(lon_row == i, both, 0.0)
        sampled[...] = picked
        return carry

    lax.fori_loop(1, HALO + 1, forward_diagonal, 0)

    kernel_slots = slots[0, 0:LEV, :]
    for k in range(probe_count):
        modeled = jnp.sum(
            kernel_slots * sampled[k * LEV : (k + 1) * LEV, :], axis=0, keepdims=True
        )
        weighted[0, k : k + 1, :] = modeled * weight_row

    def weighted_copy(side):
        return pltpu.make_async_remote_copy(
            src_ref=weighted.at[0], dst_ref=weighted.at[1 + side],
            send_sem=wt_ssem.at[side], recv_sem=wt_rsem.at[side],
            device_id=(group, (east_nbr, west_nbr)[side]), device_id_type=MESH,
        )

    for side in range(2):
        sends.append(weighted_copy(side))
        sends[-1].start()

    def inject(which, first_lon, first_ext, count):
        def body(p, carry):
            _, lon_row = columns_of(which)
            levels = slots[which, 0:LEV, :]
            prod = jnp.concatenate(
                [levels * weighted[which, k : k + 1, :] for k in range(probe_count)], axis=0
            )
            parts = []
            for q in range(2):
                parts += split_bf16(jnp.where(lon_row == first_lon + 2 * p + q, prod, 0.0))
            summed = lax.dot_general(
                jnp.concatenate(parts, axis=0), one_hot[which], (((1,), (1,)), ((), ())),
                preferred_element_type=jnp.float32,
            )
            for q in range(2):
                base = 2 * rows * q
                adj[0, first_ext + 2 * p + q] = (
                    summed[base : base + rows] + summed[base + rows : base + 2 * rows]
                )
            return carry

        lax.fori_loop(0, count // 2, body, 0)

    inject(0, 0, HALO, lon)

    gathered = jnp.zeros((n, LANES), jnp.float32)
    for k in range(probe_count):
        slot = lax.broadcasted_iota(jnp.int32, (total, LANES), 0)
        lane = lax.broadcasted_iota(jnp.int32, (total, LANES), 1)
        pick = jnp.where(lane == (slot & (CAP - 1)) + k * CAP, 1.0, 0.0)
        gathered = gathered + jnp.dot(
            jnp.where(held, weighted[0, k : k + 1, :], 0.0), pick,
            precision=HIGHEST, preferred_element_type=jnp.float32,
        )
    mis_2d[...] = gathered

    def mis_copy(target, source_id):
        return pltpu.make_async_remote_copy(
            src_ref=mis_send.at[target], dst_ref=mis_recv.at[source_id],
            send_sem=mis_ssem.at[target], recv_sem=mis_rsem.at[source_id],
            device_id=(group, target), device_id_type=MESH,
        )

    def stage_mis(i, carry):
        mis_send[i] = mis_2d[pl.ds(i, 1), :]
        return carry

    lax.fori_loop(0, n, stage_mis, 0)

    def send_mis(i, carry):
        mis_copy(lax.rem(me + i, n), me).start()
        return carry

    lax.fori_loop(1, n, send_mis, 0)

    for side in range(2):
        slot_copy(side).wait_recv()
        make_one_hot(1 + side)
    interior(backward_col)

    for side in range(2):
        weighted_copy(side).wait_recv()
    inject(1, lon - HALO, 0, HALO)
    inject(2, 0, HALO + lon, HALO)

    proj[...] = jnp.zeros_like(proj)

    def backward_diagonal(d, carry):
        diagonal(backward_col, d - 1)
        for i in (HALO - d, lon - 1 - HALO + d):
            scale = column(prior_v, 0, i)
            lowest = []
            for k in range(probe_count):
                value = (
                    column(probes_v, k * per_probe, i)
                    + scale * adj[STEPS, HALO + i, k * LEV : (k + 1) * LEV, :]
                )
                for t in range(lat // LANES):
                    hess_v[t, pl.ds(k * per_probe + i, LEV, stride=lon), :] = (
                        value[:, t * LANES : (t + 1) * LANES]
                    )
                lowest.append(value[0:1])
            surface = jnp.concatenate(lowest, axis=0)
            high = surface.astype(jnp.bfloat16).astype(jnp.float32)
            stacked = jnp.concatenate(
                [high, surface - high, jnp.zeros((16 - 2 * probe_count, lat), jnp.float32)], axis=0
            ).astype(jnp.bfloat16)
            out = jnp.dot(stacked, basis_split[i], preferred_element_type=jnp.float32)
            proj[0:probe_count, :] = proj[0:probe_count, :] + (
                out[0:probe_count, 0:LANES]
                + (out[0:probe_count, LANES:] + out[probe_count : 2 * probe_count, 0:LANES])
            )
        return carry

    lax.fori_loop(1, HALO + 1, backward_diagonal, 0)

    stores = [
        pltpu.make_async_copy(
            hess_v.at[t], hess_out.at[:, pl.ds(t * LANES, LANES)], load_sem.at[4, t]
        )
        for t in range(lat // LANES)
    ]

    def proj_copy(target, source_id):
        return pltpu.make_async_remote_copy(
            src_ref=proj, dst_ref=proj_recv.at[source_id],
            send_sem=proj_ssem.at[target], recv_sem=proj_rsem.at[source_id],
            device_id=(group, target), device_id_type=MESH,
        )

    def send_proj(i, carry):
        proj_copy(lax.rem(me + i, n), me).start()
        return carry

    lax.fori_loop(1, n, send_proj, 0)
    for store in stores:
        store.start()
    proj_recv[me] = proj[...]

    mis_recv[me] = mis_send[me]

    def mis_arrival(i, carry):
        source = lax.rem(me + i, n)
        mis_copy(source, source).wait_recv()
        return carry

    lax.fori_loop(1, n, mis_arrival, 0)

    def store_mis(i, carry):
        misfit_out[pl.ds(i, 1), :] = mis_recv[i]
        return carry

    lax.fori_loop(0, n, store_mis, 0)

    for store in stores:
        store.wait()
    for copy in sends:
        copy.wait_send()

    def finish(i, carry):
        target = lax.rem(me + i, n)
        row_copy(target, me).wait_send()
        mis_copy(target, me).wait_send()
        return carry

    lax.fori_loop(1, n, finish, 0)

    def proj_arrival(i, carry):
        source = lax.rem(me + i, n)
        proj_copy(source, source).wait_recv()
        proj_copy(source, me).wait_send()
        return carry

    lax.fori_loop(1, n, proj_arrival, 0)
    summed = lax.fori_loop(
        1, n, lambda i, acc: acc + proj_recv[i], proj_recv[0]
    )
    values = eigen_values[...]
    coeffs_out[...] = values / (1.0 + values) * summed[0:probe_count]


def local(
    probes, wind_field, prior_scale, eigen_basis, eigen_values, kernel_rows, obs_weight, tile_column
):
    probe_count, _, lon, lat = probes.shape
    rank = eigen_values.shape[0]
    n = kernel_rows.shape[0]
    rows = probe_count * LEV
    ext = lon + 2 * HALO
    total = n * CAP
    tiles = lat // LANES
    f32 = jnp.float32
    vmem = pl.BlockSpec(memory_space=pltpu.VMEM)
    anywhere = pl.BlockSpec(memory_space=pl.ANY)
    dma = pltpu.SemaphoreType.DMA
    hess, misfit, coeffs = pl.pallas_call(
        kernel,
        out_shape=(
            jax.ShapeDtypeStruct((rows * lon, lat), f32),
            jax.ShapeDtypeStruct((n, probe_count * CAP), f32),
            jax.ShapeDtypeStruct((probe_count, rank), f32),
        ),
        in_specs=[anywhere] * 4 + [vmem] * 4,
        out_specs=(anywhere, vmem, vmem),
        scratch_shapes=[
            pltpu.VMEM((tiles, rows * lon, LANES), f32),
            pltpu.VMEM((tiles, 3 * LEV * lon, LANES), f32),
            pltpu.VMEM((tiles, LEV * lon, LANES), f32),
            pltpu.VMEM((lon, lat, rank), f32),
            pltpu.VMEM((lon, lat, 2 * rank), jnp.bfloat16),
            pltpu.VMEM((tiles, rows * lon, LANES), f32),
            pltpu.VMEM((STEPS + 1, ext, rows, lat), f32),
            pltpu.VMEM((STEPS + 1, ext, rows, lat), f32),
            pltpu.VMEM((ext, LEV, lat), f32),
            pltpu.VMEM((ext, 2, LEV, lat), f32),
            pltpu.VMEM((n, 1, LEV * CAP + LANES), f32),
            pltpu.VMEM((n, 1, LEV * CAP + LANES), f32),
            pltpu.VMEM((n, LEV * CAP + LANES), f32),
            pltpu.VMEM((3, LEV + 8, total), f32),
            pltpu.VMEM((3, 8, total), f32),
            pltpu.VMEM((3, lat, total), jnp.bfloat16),
            pltpu.VMEM((rows, total), f32),
            pltpu.VMEM((n, LANES), f32),
            pltpu.VMEM((n, 1, LANES), f32),
            pltpu.VMEM((n, 1, LANES), f32),
            pltpu.VMEM((8, rank), f32),
            pltpu.VMEM((n, 8, rank), f32),
            dma((5, tiles)),
            dma((3, 2, HALO)),
            dma((3, 2, HALO)),
            dma((n,)),
            dma((n,)),
            dma((2,)),
            dma((2,)),
            dma((2,)),
            dma((2,)),
            dma((n,)),
            dma((n,)),
            dma((n,)),
            dma((n,)),
        ],
        compiler_params=pltpu.CompilerParams(
            collective_id=1, has_side_effects=True, vmem_limit_bytes=56 * 1024 * 1024
        ),
    )(
        probes.reshape(rows * lon, lat),
        wind_field.reshape(3 * LEV * lon, lat),
        prior_scale.reshape(LEV * lon, lat),
        eigen_basis,
        eigen_values.reshape(1, rank),
        kernel_rows,
        obs_weight,
        tile_column,
    )
    return hess.reshape(probes.shape), misfit, coeffs


def solution(mesh):
    in_specs = (
        P("groups", None, "cells", None),
        P(None, None, "cells", None),
        P(None, "cells", None),
        P("cells", None, None),
        P(),
        P(("groups", "cells"), None),
        P(("groups", "cells"), None),
        P(("groups", "cells"), None),
    )
    out_specs = (P("groups", None, "cells", None), P(("groups", "cells"), None), P("groups", None))
    return jax.shard_map(local, mesh=mesh, in_specs=in_specs, out_specs=out_specs, check_vma=False)
```

```python
import functools

import jax
import jax.numpy as jnp
from jax import lax
from jax.experimental import pallas as pl
from jax.experimental.pallas import tpu as pltpu
from jax.sharding import PartitionSpec as P

MESH = pl.DeviceIdType.MESH
HIGHEST = lax.Precision.HIGHEST
LEV = 16
STEPS = 4
CAP = 32
LANES = 128
HALO = STEPS


def split_bf16(value):
    high = value.astype(jnp.bfloat16)
    low = (value - high.astype(jnp.float32)).astype(jnp.bfloat16)
    return high, low


def kernel(
    probes, wind, prior, basis, eigen_values, kernel_rows, obs_weight, tile_column,
    hess_out, misfit_out, coeffs_out,
    probes_v, wind_v, prior_v, basis_v, basis_split, hess_v, to_inner, to_outer,
    fwd, adj, east, north_mix, row_send, row_recv, rows_2d, slots, weighted, one_hot, sampled,
    mis_2d, mis_send, mis_recv, proj, proj_recv,
    load_sem, col_send, col_recv, row_ssem, row_rsem, slot_ssem, slot_rsem, wt_ssem, wt_rsem,
    mis_ssem, mis_rsem, proj_ssem, proj_rsem,
):
    group = lax.axis_index("groups")
    me = lax.axis_index("cells")
    n = lax.axis_size("cells")
    east_nbr = lax.rem(me + 1, n)
    west_nbr = lax.rem(me + n - 1, n)
    lat = probes.shape[1]
    lon = fwd[0].shape[0] - 2 * HALO
    probe_count = fwd[0].shape[2] // LEV
    rows = probe_count * LEV
    tiles = lat // LANES
    total = n * CAP
    per_probe = LEV * lon

    barrier = pltpu.get_barrier_semaphore()

    def greet(i, carry):
        pl.semaphore_signal(
            barrier, inc=1, device_id=(group, lax.rem(me + i, n)), device_id_type=MESH
        )
        return carry

    lax.fori_loop(1, n, greet, 0)

    def tile_loads(source, target, at):
        return [
            pltpu.make_async_copy(
                source.at[:, pl.ds(t * LANES, LANES)], target.at[t], load_sem.at[at, t]
            )
            for t in range(tiles)
        ]

    loads = [
        tile_loads(prior, prior_v, 0),
        tile_loads(probes, probes_v, 1),
        tile_loads(wind, wind_v, 2),
        [pltpu.make_async_copy(basis, basis_v, load_sem.at[3, 0])],
    ]
    for load in loads:
        for piece in load:
            piece.start()

    def wait_loads(at):
        for piece in loads[at]:
            piece.wait()

    def column(ref, base, i):
        return jnp.concatenate(
            [ref[t, pl.ds(base + i, LEV, stride=lon), :] for t in range(tiles)], axis=1
        )

    def stage_row(i, carry):
        row_send[i, :, 0 : LEV * CAP] = kernel_rows[pl.ds(i, 1), :]
        row_send[i, :, LEV * CAP : LEV * CAP + CAP] = obs_weight[pl.ds(i, 1), :]
        row_send[i, :, LEV * CAP + CAP :] = jnp.zeros((1, LANES - CAP), jnp.float32)
        return carry

    lax.fori_loop(0, n, stage_row, 0)

    wait_loads(0)
    wait_loads(1)

    first = lax.broadcasted_iota(jnp.int32, (lat, lat), 0)
    second = lax.broadcasted_iota(jnp.int32, (lat, lat), 1)

    def latitude(place):
        return tiles * (place & (LANES - 1)) + (place >> (LANES.bit_length() - 1))

    to_inner[...] = jnp.where(first == latitude(second), 1.0, 0.0).astype(jnp.bfloat16)
    to_outer[...] = jnp.where(second == latitude(first), 1.0, 0.0).astype(jnp.bfloat16)

    def permuted(blocks, order):
        stacked = jnp.concatenate(blocks, axis=0)
        height = stacked.shape[0]
        moved = jnp.dot(
            jnp.concatenate(split_bf16(stacked), axis=0), order[...],
            preferred_element_type=jnp.float32,
        )
        return moved[:height] + moved[height:]

    def tile(value, t):
        return value[:, t * LANES : (t + 1) * LANES]

    wait_loads(2)

    def load_pair(d, carry):
        pair = (lon - 1 - d, d)
        blocks = []
        for i in pair:
            scale = column(prior_v, 0, i)
            for k in range(probe_count):
                blocks.append(scale * column(probes_v, k * per_probe, i))
            blocks += [column(wind_v, c * per_probe, i) for c in range(3)]
        inner = permuted(blocks, to_inner)
        level = lax.broadcasted_iota(jnp.int32, (LEV, LANES), 0)
        lane = lax.broadcasted_iota(jnp.int32, (LEV, LANES), 1)
        for at, i in enumerate(pair):
            base = at * (rows + 3 * LEV)
            for t in range(tiles):
                part = tile(inner[base : base + rows + 3 * LEV], t)
                fwd[0][HALO + i, t] = part[:rows]
                east[HALO + i, t] = 0.3 * part[rows : rows + LEV]
                north = 0.15 * part[rows + LEV : rows + 2 * LEV]
                north_mix[HALO + i, 0, t] = jnp.where(lane == 0, 0.0, north) if t == 0 else north
                north_mix[HALO + i, 1, t] = jnp.where(
                    level == 0, 0.0, 0.025 * (1.0 + part[rows + 2 * LEV :])
                )
        return carry

    lax.fori_loop(0, HALO, load_pair, 0)

    pl.semaphore_wait(barrier, n - 1)

    def row_copy(target, source_id):
        return pltpu.make_async_remote_copy(
            src_ref=row_send.at[target], dst_ref=row_recv.at[source_id],
            send_sem=row_ssem.at[target], recv_sem=row_rsem.at[source_id],
            device_id=(group, target), device_id_type=MESH,
        )

    def send_row(i, carry):
        row_copy(lax.rem(me + i, n), me).start()
        return carry

    lax.fori_loop(1, n, send_row, 0)

    arrays = (fwd[0], east, north_mix)

    def column_copy(kind, side, d):
        if side == 0:
            source, target, device = HALO + lon - 1 - d, HALO - 1 - d, east_nbr
        else:
            source, target, device = HALO + d, HALO + lon + d, west_nbr
        return pltpu.make_async_remote_copy(
            src_ref=arrays[kind].at[source], dst_ref=arrays[kind].at[target],
            send_sem=col_send.at[kind, side, d], recv_sem=col_recv.at[kind, side, d],
            device_id=(group, device), device_id_type=MESH,
        )

    sends = []
    for d in range(HALO):
        for kind in range(3):
            if kind == 2 and d == HALO - 1:
                continue
            for side in range(2):
                if kind == 1 and d == HALO - 1 and side == 0:
                    continue
                sends.append(column_copy(kind, side, d))
                sends[-1].start()

    def shifted_levels(ref, s, e, t, k, center):
        if k > 0:
            below = ref[s][e, t, pl.ds(k * LEV - 1, LEV), :]
        else:
            below = pltpu.roll(center, 1, 0)
        if k < probe_count - 1:
            above = ref[s][e, t, pl.ds(k * LEV + 1, LEV), :]
        else:
            above = pltpu.roll(center, LEV - 1, 0)
        return below, above

    def mixed(ref, s, e, t, k, center, mixing, mixing_above):
        below, above = shifted_levels(ref, s, e, t, k, center)
        return mixing * (below - center) - mixing_above * (center - above)

    def forward_col(s, e):
        for t in range(tiles):
            east_here = east[e, t]
            east_next = east[e + 1, t]
            north = north_mix[e, 0, t]
            after = (t + 1) % tiles
            north_after = north_mix[e, 0, after]
            if t == tiles - 1:
                north_after = pltpu.roll(north_after, LANES - 1, 1)
            mixing = north_mix[e, 1, t]
            mixing_above = pltpu.roll(mixing, LEV - 1, 0)
            for k in range(probe_count):
                part = pl.ds(k * LEV, LEV)
                center = fwd[s][e, t, part, :]
                flux = east_here * jnp.where(east_here > 0.0, fwd[s][e - 1, t, part, :], center)
                flux_next = east_next * jnp.where(
                    east_next > 0.0, center, fwd[s][e + 1, t, part, :]
                )
                before = fwd[s][e, (t - 1) % tiles, part, :]
                if t == 0:
                    before = pltpu.roll(before, 1, 1)
                south = north * jnp.where(north > 0.0, before, center)
                behind = fwd[s][e, after, part, :]
                if t == tiles - 1:
                    behind = pltpu.roll(behind, LANES - 1, 1)
                south_next = north_after * jnp.where(north_after > 0.0, center, behind)
                fwd[s + 1][e, t, part, :] = (
                    center - (flux_next - flux) - (south_next - south)
                    + mixed(fwd, s, e, t, k, center, mixing, mixing_above)
                )

    def backward_col(s, e):
        for t in range(tiles):
            east_neg = jnp.minimum(east[e, t], 0.0)
            east_pos = jnp.maximum(east[e + 1, t], 0.0)
            after = (t + 1) % tiles
            north_neg = jnp.minimum(north_mix[e, 0, t], 0.0)
            north_after = jnp.maximum(north_mix[e, 0, after], 0.0)
            if t == tiles - 1:
                north_after = pltpu.roll(north_after, LANES - 1, 1)
            mixing = north_mix[e, 1, t]
            mixing_above = pltpu.roll(mixing, LEV - 1, 0)
            for k in range(probe_count):
                part = pl.ds(k * LEV, LEV)
                center = adj[s][e, t, part, :]
                before = adj[s][e, (t - 1) % tiles, part, :]
                if t == 0:
                    before = pltpu.roll(before, 1, 1)
                behind = adj[s][e, after, part, :]
                if t == tiles - 1:
                    behind = pltpu.roll(behind, LANES - 1, 1)
                adj[s + 1][e, t, part, :] = (
                    center
                    + east_pos * (adj[s][e + 1, t, part, :] - center)
                    + east_neg * (center - adj[s][e - 1, t, part, :])
                    + north_after * (behind - center) + north_neg * (center - before)
                    + mixed(adj, s, e, t, k, center, mixing, mixing_above)
                )

    def interior(col):
        for s in range(STEPS - 1):
            def body(i, carry, s=s):
                col(s, HALO + i)
                return carry

            lax.fori_loop(s + 1, lon - 1 - s, body, 0)

    def diagonal(col, d):
        for s in range(STEPS):
            col(s, HALO - d + s)
            col(s, HALO + lon - 1 + d - s)

    interior(forward_col)

    row_recv[me] = row_send[me]

    def row_arrival(i, carry):
        source = lax.rem(me + i, n)
        row_copy(source, source).wait_recv()
        return carry

    lax.fori_loop(1, n, row_arrival, 0)

    def flatten_row(i, carry):
        rows_2d[pl.ds(i, 1), :] = row_recv[i]
        return carry

    lax.fori_loop(0, n, flatten_row, 0)

    slot_id = lax.broadcasted_iota(jnp.int32, (n, total), 1)
    holder = lax.broadcasted_iota(jnp.int32, (n, total), 0)
    held = (slot_id >> 5) == holder

    def spread(block, offset):
        lane = lax.broadcasted_iota(jnp.int32, (block.shape[1], total), 0)
        slot = lax.broadcasted_iota(jnp.int32, (block.shape[1], total), 1)
        pick = jnp.where(lane == (slot & (CAP - 1)) + offset, 1.0, 0.0)
        wide = jnp.dot(block, pick, precision=HIGHEST, preferred_element_type=jnp.float32)
        return jnp.sum(jnp.where(held, wide, 0.0), axis=0, keepdims=True)

    for level in range(LEV):
        at = level * CAP // LANES
        slots[0, level : level + 1, :] = spread(
            rows_2d[:, at * LANES : (at + 1) * LANES], level * CAP % LANES
        )
    weight_row = spread(rows_2d[:, LEV * CAP :], 0)
    slots[0, LEV : LEV + 1, :] = spread(tile_column[...].astype(jnp.float32), 0)
    slots[0, LEV + 1 :, :] = jnp.zeros((slots.shape[1] - LEV - 1, total), jnp.float32)

    def slot_copy(side):
        return pltpu.make_async_remote_copy(
            src_ref=slots.at[0], dst_ref=slots.at[1 + side],
            send_sem=slot_ssem.at[side], recv_sem=slot_rsem.at[side],
            device_id=(group, (east_nbr, west_nbr)[side]), device_id_type=MESH,
        )

    for side in range(2):
        sends.append(slot_copy(side))
        sends[-1].start()

    def columns_of(which):
        column = slots[which, LEV : LEV + 1, :].astype(jnp.int32)
        return column, column >> (lat.bit_length() - 1)

    def make_one_hot(which):
        column, _ = columns_of(which)
        row = jnp.where(column < 0, -1, column & (lat - 1))
        place = latitude(lax.broadcasted_iota(jnp.int32, (lat, total), 0))
        one_hot[which] = jnp.where(place == row, 1.0, 0.0).astype(jnp.bfloat16)

    make_one_hot(0)
    sampled[...] = jnp.zeros_like(sampled)
    wait_loads(3)

    def split_basis(i, carry):
        high, low = split_bf16(basis_v[i])
        basis_split[i, :, 0:LANES] = high
        basis_split[i, :, LANES:] = low
        return carry

    lax.fori_loop(0, lon, split_basis, 0)

    def forward_diagonal(d, carry):
        for side in range(2):
            pltpu.make_async_remote_copy(
                src_ref=fwd[0].at[0], dst_ref=fwd[0].at[0],
                send_sem=col_send.at[0, side, d - 1], recv_sem=col_recv.at[0, side, d - 1],
                device_id=(group, east_nbr), device_id_type=MESH,
            ).wait_recv()

        def wait_wind(kind, side, at):
            pltpu.make_async_remote_copy(
                src_ref=arrays[kind].at[0], dst_ref=arrays[kind].at[0],
                send_sem=col_send.at[kind, side, at], recv_sem=col_recv.at[kind, side, at],
                device_id=(group, east_nbr), device_id_type=MESH,
            ).wait_recv()

        wait_wind(1, 1, d - 1)

        @pl.when(d > 1)
        def _():
            wait_wind(1, 0, d - 2)
            wait_wind(2, 0, d - 2)
            wait_wind(2, 1, d - 2)

        diagonal(forward_col, d - 1)
        pair = (HALO - d, lon - 1 - HALO + d)
        parts = []
        for i in pair:
            parts += split_bf16(
                jnp.concatenate([fwd[STEPS][HALO + i, t] for t in range(tiles)], axis=1)
            )
        found = jnp.dot(
            jnp.concatenate(parts, axis=0), one_hot[0], preferred_element_type=jnp.float32
        )
        _, lon_row = columns_of(0)
        picked = sampled[...]
        for at, i in enumerate(pair):
            base = 2 * rows * at
            both = found[base : base + rows] + found[base + rows : base + 2 * rows]
            picked = picked + jnp.where(lon_row == i, both, 0.0)
        sampled[...] = picked
        return carry

    lax.fori_loop(1, HALO + 1, forward_diagonal, 0)

    kernel_slots = slots[0, 0:LEV, :]
    for k in range(probe_count):
        modeled = jnp.sum(
            kernel_slots * sampled[k * LEV : (k + 1) * LEV, :], axis=0, keepdims=True
        )
        weighted[0, k : k + 1, :] = modeled * weight_row

    def weighted_copy(side):
        return pltpu.make_async_remote_copy(
            src_ref=weighted.at[0], dst_ref=weighted.at[1 + side],
            send_sem=wt_ssem.at[side], recv_sem=wt_rsem.at[side],
            device_id=(group, (east_nbr, west_nbr)[side]), device_id_type=MESH,
        )

    for side in range(2):
        sends.append(weighted_copy(side))
        sends[-1].start()

    def inject(which, first_lon, first_ext, count):
        def body(p, carry):
            _, lon_row = columns_of(which)
            levels = slots[which, 0:LEV, :]
            prod = jnp.concatenate(
                [levels * weighted[which, k : k + 1, :] for k in range(probe_count)], axis=0
            )
            parts = []
            for q in range(2):
                parts += split_bf16(jnp.where(lon_row == first_lon + 2 * p + q, prod, 0.0))
            summed = lax.dot_general(
                jnp.concatenate(parts, axis=0), one_hot[which], (((1,), (1,)), ((), ())),
                preferred_element_type=jnp.float32,
            )
            for q in range(2):
                base = 2 * rows * q
                both = summed[base : base + rows] + summed[base + rows : base + 2 * rows]
                for t in range(tiles):
                    adj[0][first_ext + 2 * p + q, t] = tile(both, t)
            return carry

        lax.fori_loop(0, count // 2, body, 0)

    inject(0, 0, HALO, lon)

    gathered = jnp.zeros((n, LANES), jnp.float32)
    for k in range(probe_count):
        slot = lax.broadcasted_iota(jnp.int32, (total, LANES), 0)
        lane = lax.broadcasted_iota(jnp.int32, (total, LANES), 1)
        pick = jnp.where(lane == (slot & (CAP - 1)) + k * CAP, 1.0, 0.0)
        gathered = gathered + jnp.dot(
            jnp.where(held, weighted[0, k : k + 1, :], 0.0), pick,
            precision=HIGHEST, preferred_element_type=jnp.float32,
        )
    mis_2d[...] = gathered

    def mis_copy(target, source_id):
        return pltpu.make_async_remote_copy(
            src_ref=mis_send.at[target], dst_ref=mis_recv.at[source_id],
            send_sem=mis_ssem.at[target], recv_sem=mis_rsem.at[source_id],
            device_id=(group, target), device_id_type=MESH,
        )

    def stage_mis(i, carry):
        mis_send[i] = mis_2d[pl.ds(i, 1), :]
        return carry

    lax.fori_loop(0, n, stage_mis, 0)

    def send_mis(i, carry):
        mis_copy(lax.rem(me + i, n), me).start()
        return carry

    lax.fori_loop(1, n, send_mis, 0)

    for side in range(2):
        slot_copy(side).wait_recv()
        make_one_hot(1 + side)
    interior(backward_col)

    for side in range(2):
        weighted_copy(side).wait_recv()
    inject(1, lon - HALO, 0, HALO)
    inject(2, 0, HALO + lon, HALO)

    proj[...] = jnp.zeros_like(proj)

    def backward_diagonal(d, carry):
        diagonal(backward_col, d - 1)
        pair = (HALO - d, lon - 1 - HALO + d)
        pulled = permuted(
            [
                jnp.concatenate([adj[STEPS][HALO + i, t] for t in range(tiles)], axis=1)
                for i in pair
            ],
            to_outer,
        )
        for at, i in enumerate(pair):
            scale = column(prior_v, 0, i)
            lowest = []
            for k in range(probe_count):
                value = (
                    column(probes_v, k * per_probe, i)
                    + scale * pulled[at * rows + k * LEV : at * rows + (k + 1) * LEV]
                )
                for t in range(tiles):
                    hess_v[t, pl.ds(k * per_probe + i, LEV, stride=lon), :] = tile(value, t)
                lowest.append(value[0:1])
            surface = jnp.concatenate(lowest, axis=0)
            high = surface.astype(jnp.bfloat16).astype(jnp.float32)
            stacked = jnp.concatenate(
                [high, surface - high, jnp.zeros((16 - 2 * probe_count, lat), jnp.float32)], axis=0
            ).astype(jnp.bfloat16)
            out = jnp.dot(stacked, basis_split[i], preferred_element_type=jnp.float32)
            proj[0:probe_count, :] = proj[0:probe_count, :] + (
                out[0:probe_count, 0:LANES]
                + (out[0:probe_count, LANES:] + out[probe_count : 2 * probe_count, 0:LANES])
            )
        return carry

    lax.fori_loop(1, HALO + 1, backward_diagonal, 0)

    stores = [
        pltpu.make_async_copy(
            hess_v.at[t], hess_out.at[:, pl.ds(t * LANES, LANES)], load_sem.at[4, t]
        )
        for t in range(tiles)
    ]

    def proj_copy(target, source_id):
        return pltpu.make_async_remote_copy(
            src_ref=proj, dst_ref=proj_recv.at[source_id],
            send_sem=proj_ssem.at[target], recv_sem=proj_rsem.at[source_id],
            device_id=(group, target), device_id_type=MESH,
        )

    def send_proj(i, carry):
        proj_copy(lax.rem(me + i, n), me).start()
        return carry

    lax.fori_loop(1, n, send_proj, 0)
    for store in stores:
        store.start()
    proj_recv[me] = proj[...]

    mis_recv[me] = mis_send[me]

    def mis_arrival(i, carry):
        source = lax.rem(me + i, n)
        mis_copy(source, source).wait_recv()
        return carry

    lax.fori_loop(1, n, mis_arrival, 0)

    def store_mis(i, carry):
        misfit_out[pl.ds(i, 1), :] = mis_recv[i]
        return carry

    lax.fori_loop(0, n, store_mis, 0)

    for store in stores:
        store.wait()
    for copy in sends:
        copy.wait_send()

    def finish(i, carry):
        target = lax.rem(me + i, n)
        row_copy(target, me).wait_send()
        mis_copy(target, me).wait_send()
        return carry

    lax.fori_loop(1, n, finish, 0)

    def proj_arrival(i, carry):
        source = lax.rem(me + i, n)
        proj_copy(source, source).wait_recv()
        proj_copy(source, me).wait_send()
        return carry

    lax.fori_loop(1, n, proj_arrival, 0)
    summed = lax.fori_loop(
        1, n, lambda i, acc: acc + proj_recv[i], proj_recv[0]
    )
    values = eigen_values[...]
    coeffs_out[...] = values / (1.0 + values) * summed[0:probe_count]


def finish_kernel(hess, misfit, coeffs, hess_out, misfit_out, coeffs_out):
    hess_out[...] = hess[...]
    misfit_out[...] = misfit[...]
    coeffs_out[...] = coeffs[...]


def local(
    probes, wind_field, prior_scale, eigen_basis, eigen_values, kernel_rows, obs_weight, tile_column
):
    probe_count, _, lon, lat = probes.shape
    rank = eigen_values.shape[0]
    n = kernel_rows.shape[0]
    rows = probe_count * LEV
    ext = lon + 2 * HALO
    total = n * CAP
    tiles = lat // LANES
    f32 = jnp.float32
    vmem = pl.BlockSpec(memory_space=pltpu.VMEM)
    anywhere = pl.BlockSpec(memory_space=pl.ANY)
    dma = pltpu.SemaphoreType.DMA
    hess, misfit, coeffs = pl.pallas_call(
        kernel,
        out_shape=(
            jax.ShapeDtypeStruct((rows * lon, lat), f32),
            jax.ShapeDtypeStruct((n, probe_count * CAP), f32),
            jax.ShapeDtypeStruct((probe_count, rank), f32),
        ),
        in_specs=[anywhere] * 4 + [vmem] * 4,
        out_specs=(anywhere, vmem, vmem),
        scratch_shapes=[
            pltpu.VMEM((tiles, rows * lon, LANES), f32),
            pltpu.VMEM((tiles, 3 * LEV * lon, LANES), f32),
            pltpu.VMEM((tiles, LEV * lon, LANES), f32),
            pltpu.VMEM((lon, lat, rank), f32),
            pltpu.VMEM((lon, lat, 2 * rank), jnp.bfloat16),
            pltpu.VMEM((tiles, rows * lon, LANES), f32),
            pltpu.VMEM((lat, lat), jnp.bfloat16),
            pltpu.VMEM((lat, lat), jnp.bfloat16),
            (pltpu.VMEM((ext, tiles, rows, LANES), f32),) * (STEPS + 1),
            (pltpu.VMEM((ext, tiles, rows, LANES), f32),) * (STEPS + 1),
            pltpu.VMEM((ext, tiles, LEV, LANES), f32),
            pltpu.VMEM((ext, 2, tiles, LEV, LANES), f32),
            pltpu.VMEM((n, 1, LEV * CAP + LANES), f32),
            pltpu.VMEM((n, 1, LEV * CAP + LANES), f32),
            pltpu.VMEM((n, LEV * CAP + LANES), f32),
            pltpu.VMEM((3, LEV + 8, total), f32),
            pltpu.VMEM((3, 8, total), f32),
            pltpu.VMEM((3, lat, total), jnp.bfloat16),
            pltpu.VMEM((rows, total), f32),
            pltpu.VMEM((n, LANES), f32),
            pltpu.VMEM((n, 1, LANES), f32),
            pltpu.VMEM((n, 1, LANES), f32),
            pltpu.VMEM((8, rank), f32),
            pltpu.VMEM((n, 8, rank), f32),
            dma((5, tiles)),
            dma((3, 2, HALO)),
            dma((3, 2, HALO)),
            dma((n,)),
            dma((n,)),
            dma((2,)),
            dma((2,)),
            dma((2,)),
            dma((2,)),
            dma((n,)),
            dma((n,)),
            dma((n,)),
            dma((n,)),
        ],
        compiler_params=pltpu.CompilerParams(
            collective_id=1, has_side_effects=True, vmem_limit_bytes=56 * 1024 * 1024
        ),
    )(
        probes.reshape(rows * lon, lat),
        wind_field.reshape(3 * LEV * lon, lat),
        prior_scale.reshape(LEV * lon, lat),
        eigen_basis,
        eigen_values.reshape(1, rank),
        kernel_rows,
        obs_weight,
        tile_column,
    )
    hess, misfit, coeffs = pl.pallas_call(
        finish_kernel,
        out_shape=tuple(jax.ShapeDtypeStruct(x.shape, f32) for x in (hess, misfit, coeffs)),
        in_specs=[vmem] * 3,
        out_specs=(vmem,) * 3,
    )(hess, misfit, coeffs)
    return hess.reshape(probes.shape), misfit, coeffs


def solution(mesh):
    in_specs = (
        P("groups", None, "cells", None),
        P(None, None, "cells", None),
        P(None, "cells", None),
        P("cells", None, None),
        P(),
        P(("groups", "cells"), None),
        P(("groups", "cells"), None),
        P(("groups", "cells"), None),
    )
    out_specs = (P("groups", None, "cells", None), P(("groups", "cells"), None), P("groups", None))
    return jax.shard_map(local, mesh=mesh, in_specs=in_specs, out_specs=out_specs, check_vma=False)
```

```python
import functools

import jax
import jax.numpy as jnp
from jax import lax
from jax.experimental import pallas as pl
from jax.experimental.pallas import tpu as pltpu
from jax.sharding import PartitionSpec as P

MESH = pl.DeviceIdType.MESH
HIGHEST = lax.Precision.HIGHEST
LEV = 16
STEPS = 4
CAP = 32
LANES = 128
HALO = STEPS


def split_bf16(value):
    high = value.astype(jnp.bfloat16)
    low = (value - high.astype(jnp.float32)).astype(jnp.bfloat16)
    return high, low


def kernel(
    probes, wind, prior, basis, eigen_values, kernel_rows, obs_weight, tile_column,
    hess_out, misfit_out, coeffs_out,
    probes_v, wind_v, prior_v, basis_v, basis_split, hess_v, to_inner, to_outer, surface,
    fwd, adj, rates, row_send, row_recv, rows_2d, slots, weighted, one_hot, sampled,
    mis_2d, mis_send, mis_recv, proj, proj_recv,
    load_sem, col_send, col_recv, row_ssem, row_rsem, slot_ssem, slot_rsem, wt_ssem, wt_rsem,
    mis_ssem, mis_rsem, proj_ssem, proj_rsem, hand_ssem, hand_rsem,
):
    group = lax.axis_index("groups")
    me = lax.axis_index("cells")
    n = lax.axis_size("cells")
    group_count = lax.axis_size("groups")
    east_nbr = lax.rem(me + 1, n)
    west_nbr = lax.rem(me + n - 1, n)
    lat = probes.shape[1]
    lon = fwd[0].shape[0] - 2 * HALO
    probe_count = fwd[0].shape[2] // LEV
    rows = probe_count * LEV
    tiles = lat // LANES
    total = n * CAP
    per_probe = LEV * lon

    barrier = pltpu.get_barrier_semaphore()

    def greet(i, carry):
        pl.semaphore_signal(
            barrier, inc=1, device_id=(group, lax.rem(me + i, n)), device_id_type=MESH
        )
        return carry

    lax.fori_loop(1, n, greet, 0)
    for o in range(1, group_count):
        pl.semaphore_signal(
            barrier, inc=1, device_id=(lax.rem(group + o, group_count), me), device_id_type=MESH
        )

    def tile_loads(source, target, at):
        return [
            pltpu.make_async_copy(
                source.at[:, pl.ds(t * LANES, LANES)], target.at[t], load_sem.at[at, t]
            )
            for t in range(tiles)
        ]

    loads = [
        tile_loads(prior, prior_v, 0),
        tile_loads(probes, probes_v, 1),
        tile_loads(wind, wind_v, 2),
        [pltpu.make_async_copy(basis, basis_v, load_sem.at[3, 0])],
    ]
    for load in loads:
        for piece in load:
            piece.start()

    def wait_loads(at):
        for piece in loads[at]:
            piece.wait()

    def column(ref, base, i):
        return jnp.concatenate(
            [ref[t, pl.ds(base + i, LEV, stride=lon), :] for t in range(tiles)], axis=1
        )

    def stage_row(i, carry):
        row_send[i, :, 0 : LEV * CAP] = kernel_rows[pl.ds(i, 1), :]
        row_send[i, :, LEV * CAP : LEV * CAP + CAP] = obs_weight[pl.ds(i, 1), :]
        row_send[i, :, LEV * CAP + CAP :] = jnp.zeros((1, LANES - CAP), jnp.float32)
        return carry

    lax.fori_loop(0, n, stage_row, 0)

    wait_loads(0)
    wait_loads(1)

    first = lax.broadcasted_iota(jnp.int32, (lat, lat), 0)
    second = lax.broadcasted_iota(jnp.int32, (lat, lat), 1)

    def latitude(place):
        return tiles * (place & (LANES - 1)) + (place >> (LANES.bit_length() - 1))

    to_inner[...] = jnp.where(first == latitude(second), 1.0, 0.0).astype(jnp.bfloat16)
    to_outer[...] = jnp.where(second == latitude(first), 1.0, 0.0).astype(jnp.bfloat16)

    def permuted(blocks, order):
        stacked = jnp.concatenate(blocks, axis=0)
        height = stacked.shape[0]
        moved = jnp.dot(
            jnp.concatenate(split_bf16(stacked), axis=0), order[...],
            preferred_element_type=jnp.float32,
        )
        return moved[:height] + moved[height:]

    def tile(value, t):
        return value[:, t * LANES : (t + 1) * LANES]

    wait_loads(2)

    def load_pair(d, carry):
        pair = (lon - 1 - d, d)
        blocks = []
        for i in pair:
            scale = column(prior_v, 0, i)
            for k in range(probe_count):
                blocks.append(scale * column(probes_v, k * per_probe, i))
            blocks += [column(wind_v, c * per_probe, i) for c in range(3)]
        inner = permuted(blocks, to_inner)
        level = lax.broadcasted_iota(jnp.int32, (LEV, LANES), 0)
        lane = lax.broadcasted_iota(jnp.int32, (LEV, LANES), 1)
        for at, i in enumerate(pair):
            base = at * (rows + 3 * LEV)
            for t in range(tiles):
                part = tile(inner[base : base + rows + 3 * LEV], t)
                fwd[0][HALO + i, t] = part[:rows]
                rates[HALO + i, t, 0] = 0.3 * part[rows : rows + LEV]
                north = 0.15 * part[rows + LEV : rows + 2 * LEV]
                rates[HALO + i, t, 1] = jnp.where(lane == 0, 0.0, north) if t == 0 else north
                rates[HALO + i, t, 2] = jnp.where(
                    level == 0, 0.0, 0.025 * (1.0 + part[rows + 2 * LEV :])
                )
        return carry

    lax.fori_loop(0, HALO, load_pair, 0)

    pl.semaphore_wait(barrier, n - 1 + group_count - 1)

    def row_copy(target, source_id):
        return pltpu.make_async_remote_copy(
            src_ref=row_send.at[target], dst_ref=row_recv.at[source_id],
            send_sem=row_ssem.at[target], recv_sem=row_rsem.at[source_id],
            device_id=(group, target), device_id_type=MESH,
        )

    def send_row(i, carry):
        row_copy(lax.rem(me + i, n), me).start()
        return carry

    lax.fori_loop(1, n, send_row, 0)

    share = tiles // group_count

    def places(side, d):
        if side == 0:
            return HALO + lon - 1 - d, HALO - 1 - d, east_nbr
        return HALO + d, HALO + lon + d, west_nbr

    def rate_part(e, d, owner):
        if d < HALO - 1:
            return rates.at[e, pl.ds(owner * share, share)]
        return rates.at[e, pl.ds(owner * share, share), 0]

    def tracer_copy(side, d):
        source, target, device = places(side, d)
        return pltpu.make_async_remote_copy(
            src_ref=fwd[0].at[source], dst_ref=fwd[0].at[target],
            send_sem=col_send.at[0, side, d], recv_sem=col_recv.at[0, side, d],
            device_id=(group, device), device_id_type=MESH,
        )

    def rate_copy(side, d):
        source, target, device = places(side, d)
        return pltpu.make_async_remote_copy(
            src_ref=rate_part(source, d, group), dst_ref=rate_part(target, d, group),
            send_sem=col_send.at[1, side, d], recv_sem=col_recv.at[1, side, d],
            device_id=(group, device), device_id_type=MESH,
        )

    sends = []
    rate_plan = [(side, d) for d in range(HALO) for side in range(2) if d < HALO - 1 or side == 1]
    for side, d in rate_plan:
        sends.append(rate_copy(side, d))
        sends[-1].start()
    for d in range(HALO):
        for side in range(2):
            sends.append(tracer_copy(side, d))
            sends[-1].start()

    def hand_on(at):
        for side, d in rate_plan:
            if d != at:
                continue
            rate_copy(side, d).wait_recv()
            part = rate_part(places(side, d)[1], d, group)
            for o in range(1, group_count):
                peer = lax.rem(group + o, group_count)
                sends.append(
                    pltpu.make_async_remote_copy(
                        src_ref=part, dst_ref=part,
                        send_sem=hand_ssem.at[side, d, peer],
                        recv_sem=hand_rsem.at[side, d, group],
                        device_id=(peer, me), device_id_type=MESH,
                    )
                )
                sends[-1].start()

    def shifted_levels(ref, s, e, t, k, center):
        if k > 0:
            below = ref[s][e, t, pl.ds(k * LEV - 1, LEV), :]
        else:
            below = pltpu.roll(center, 1, 0)
        if k < probe_count - 1:
            above = ref[s][e, t, pl.ds(k * LEV + 1, LEV), :]
        else:
            above = pltpu.roll(center, LEV - 1, 0)
        return below, above

    def mixed(ref, s, e, t, k, center, mixing, mixing_above):
        below, above = shifted_levels(ref, s, e, t, k, center)
        return mixing * (below - center) - mixing_above * (center - above)

    def forward_col(s, e):
        for t in range(tiles):
            east_here = rates[e, t, 0]
            east_next = rates[e + 1, t, 0]
            north = rates[e, t, 1]
            after = (t + 1) % tiles
            north_after = rates[e, after, 1]
            if t == tiles - 1:
                north_after = pltpu.roll(north_after, LANES - 1, 1)
            mixing = rates[e, t, 2]
            mixing_above = pltpu.roll(mixing, LEV - 1, 0)
            for k in range(probe_count):
                part = pl.ds(k * LEV, LEV)
                center = fwd[s][e, t, part, :]
                flux = east_here * jnp.where(east_here > 0.0, fwd[s][e - 1, t, part, :], center)
                flux_next = east_next * jnp.where(
                    east_next > 0.0, center, fwd[s][e + 1, t, part, :]
                )
                before = fwd[s][e, (t - 1) % tiles, part, :]
                if t == 0:
                    before = pltpu.roll(before, 1, 1)
                south = north * jnp.where(north > 0.0, before, center)
                behind = fwd[s][e, after, part, :]
                if t == tiles - 1:
                    behind = pltpu.roll(behind, LANES - 1, 1)
                south_next = north_after * jnp.where(north_after > 0.0, center, behind)
                fwd[s + 1][e, t, part, :] = (
                    center - (flux_next - flux) - (south_next - south)
                    + mixed(fwd, s, e, t, k, center, mixing, mixing_above)
                )

    def backward_col(s, e):
        for t in range(tiles):
            east_neg = jnp.minimum(rates[e, t, 0], 0.0)
            east_pos = jnp.maximum(rates[e + 1, t, 0], 0.0)
            after = (t + 1) % tiles
            north_neg = jnp.minimum(rates[e, t, 1], 0.0)
            north_after = jnp.maximum(rates[e, after, 1], 0.0)
            if t == tiles - 1:
                north_after = pltpu.roll(north_after, LANES - 1, 1)
            mixing = rates[e, t, 2]
            mixing_above = pltpu.roll(mixing, LEV - 1, 0)
            for k in range(probe_count):
                part = pl.ds(k * LEV, LEV)
                center = adj[s][e, t, part, :]
                before = adj[s][e, (t - 1) % tiles, part, :]
                if t == 0:
                    before = pltpu.roll(before, 1, 1)
                behind = adj[s][e, after, part, :]
                if t == tiles - 1:
                    behind = pltpu.roll(behind, LANES - 1, 1)
                adj[s + 1][e, t, part, :] = (
                    center
                    + east_pos * (adj[s][e + 1, t, part, :] - center)
                    + east_neg * (center - adj[s][e - 1, t, part, :])
                    + north_after * (behind - center) + north_neg * (center - before)
                    + mixed(adj, s, e, t, k, center, mixing, mixing_above)
                )

    def interior(col):
        for s in range(STEPS - 1):
            def body(i, carry, s=s):
                col(s, HALO + i)
                return carry

            lax.fori_loop(s + 1, lon - 1 - s, body, 0)

    def diagonal(col, d):
        for s in range(STEPS):
            col(s, HALO - d + s)
            col(s, HALO + lon - 1 + d - s)

    interior(forward_col)

    row_recv[me] = row_send[me]

    def row_arrival(i, carry):
        source = lax.rem(me + i, n)
        row_copy(source, source).wait_recv()
        return carry

    lax.fori_loop(1, n, row_arrival, 0)

    def flatten_row(i, carry):
        rows_2d[pl.ds(i, 1), :] = row_recv[i]
        return carry

    lax.fori_loop(0, n, flatten_row, 0)

    slot_id = lax.broadcasted_iota(jnp.int32, (n, total), 1)
    holder = lax.broadcasted_iota(jnp.int32, (n, total), 0)
    held = (slot_id >> 5) == holder

    def spread(block, offset):
        lane = lax.broadcasted_iota(jnp.int32, (block.shape[1], total), 0)
        slot = lax.broadcasted_iota(jnp.int32, (block.shape[1], total), 1)
        pick = jnp.where(lane == (slot & (CAP - 1)) + offset, 1.0, 0.0)
        wide = jnp.dot(block, pick, precision=HIGHEST, preferred_element_type=jnp.float32)
        return jnp.sum(jnp.where(held, wide, 0.0), axis=0, keepdims=True)

    for level in range(LEV):
        at = level * CAP // LANES
        if level % 4 == 0:
            hand_on(level // 4)
        slots[0, level : level + 1, :] = spread(
            rows_2d[:, at * LANES : (at + 1) * LANES], level * CAP % LANES
        )
    weight_row = spread(rows_2d[:, LEV * CAP :], 0)
    slots[0, LEV : LEV + 1, :] = spread(tile_column[...].astype(jnp.float32), 0)
    slots[0, LEV + 1 :, :] = jnp.zeros((slots.shape[1] - LEV - 1, total), jnp.float32)

    def slot_copy(side):
        return pltpu.make_async_remote_copy(
            src_ref=slots.at[0], dst_ref=slots.at[1 + side],
            send_sem=slot_ssem.at[side], recv_sem=slot_rsem.at[side],
            device_id=(group, (east_nbr, west_nbr)[side]), device_id_type=MESH,
        )

    for side in range(2):
        sends.append(slot_copy(side))
        sends[-1].start()

    def columns_of(which):
        column = slots[which, LEV : LEV + 1, :].astype(jnp.int32)
        return column, column >> (lat.bit_length() - 1)

    def make_one_hot(which):
        column, _ = columns_of(which)
        row = jnp.where(column < 0, -1, column & (lat - 1))
        place = latitude(lax.broadcasted_iota(jnp.int32, (lat, total), 0))
        one_hot[which] = jnp.where(place == row, 1.0, 0.0).astype(jnp.bfloat16)

    make_one_hot(0)
    sampled[...] = jnp.zeros_like(sampled)
    wait_loads(3)

    def split_basis(i, carry):
        high, low = split_bf16(basis_v[i])
        basis_split[i, :, 0:LANES] = high
        basis_split[i, :, LANES:] = low
        return carry

    lax.fori_loop(0, lon, split_basis, 0)

    def forward_diagonal(d, carry):
        def wait_for(ref, recv_sem):
            pltpu.make_async_remote_copy(
                src_ref=ref, dst_ref=ref, send_sem=col_send.at[0, 0, 0], recv_sem=recv_sem,
                device_id=(group, east_nbr), device_id_type=MESH,
            ).wait_recv()

        for side in range(2):
            wait_for(fwd[0].at[0], col_recv.at[0, side, d - 1])
        for o in range(1, group_count):
            peer = lax.rem(group + o, group_count)

            @pl.when(d < HALO)
            def _():
                for side in range(2):
                    wait_for(rates.at[0, pl.ds(0, share)], hand_rsem.at[side, d - 1, peer])

            @pl.when(d == HALO)
            def _():
                wait_for(rates.at[0, pl.ds(0, share), 0], hand_rsem.at[1, d - 1, peer])

        diagonal(forward_col, d - 1)
        pair = (HALO - d, lon - 1 - HALO + d)
        parts = []
        for i in pair:
            parts += split_bf16(
                jnp.concatenate([fwd[STEPS][HALO + i, t] for t in range(tiles)], axis=1)
            )
        found = jnp.dot(
            jnp.concatenate(parts, axis=0), one_hot[0], preferred_element_type=jnp.float32
        )
        _, lon_row = columns_of(0)
        picked = sampled[...]
        for at, i in enumerate(pair):
            base = 2 * rows * at
            both = found[base : base + rows] + found[base + rows : base + 2 * rows]
            picked = picked + jnp.where(lon_row == i, both, 0.0)
        sampled[...] = picked
        return carry

    lax.fori_loop(1, HALO + 1, forward_diagonal, 0)

    kernel_slots = slots[0, 0:LEV, :]
    for k in range(probe_count):
        modeled = jnp.sum(
            kernel_slots * sampled[k * LEV : (k + 1) * LEV, :], axis=0, keepdims=True
        )
        weighted[0, k : k + 1, :] = modeled * weight_row

    def weighted_copy(side):
        return pltpu.make_async_remote_copy(
            src_ref=weighted.at[0], dst_ref=weighted.at[1 + side],
            send_sem=wt_ssem.at[side], recv_sem=wt_rsem.at[side],
            device_id=(group, (east_nbr, west_nbr)[side]), device_id_type=MESH,
        )

    for side in range(2):
        sends.append(weighted_copy(side))
        sends[-1].start()

    def inject(which, first_lon, first_ext, count):
        def body(p, carry):
            _, lon_row = columns_of(which)
            levels = slots[which, 0:LEV, :]
            prod = jnp.concatenate(
                [levels * weighted[which, k : k + 1, :] for k in range(probe_count)], axis=0
            )
            parts = []
            for q in range(2):
                parts += split_bf16(jnp.where(lon_row == first_lon + 2 * p + q, prod, 0.0))
            summed = lax.dot_general(
                jnp.concatenate(parts, axis=0), one_hot[which], (((1,), (1,)), ((), ())),
                preferred_element_type=jnp.float32,
            )
            for q in range(2):
                base = 2 * rows * q
                both = summed[base : base + rows] + summed[base + rows : base + 2 * rows]
                for t in range(tiles):
                    adj[0][first_ext + 2 * p + q, t] = tile(both, t)
            return carry

        lax.fori_loop(0, count // 2, body, 0)

    inject(0, 0, HALO, lon)

    gathered = jnp.zeros((n, LANES), jnp.float32)
    for k in range(probe_count):
        slot = lax.broadcasted_iota(jnp.int32, (total, LANES), 0)
        lane = lax.broadcasted_iota(jnp.int32, (total, LANES), 1)
        pick = jnp.where(lane == (slot & (CAP - 1)) + k * CAP, 1.0, 0.0)
        gathered = gathered + jnp.dot(
            jnp.where(held, weighted[0, k : k + 1, :], 0.0), pick,
            precision=HIGHEST, preferred_element_type=jnp.float32,
        )
    mis_2d[...] = gathered

    def mis_copy(target, source_id):
        return pltpu.make_async_remote_copy(
            src_ref=mis_send.at[target], dst_ref=mis_recv.at[source_id],
            send_sem=mis_ssem.at[target], recv_sem=mis_rsem.at[source_id],
            device_id=(group, target), device_id_type=MESH,
        )

    def stage_mis(i, carry):
        mis_send[i] = mis_2d[pl.ds(i, 1), :]
        return carry

    lax.fori_loop(0, n, stage_mis, 0)

    def send_mis(i, carry):
        mis_copy(lax.rem(me + i, n), me).start()
        return carry

    lax.fori_loop(1, n, send_mis, 0)

    for side in range(2):
        slot_copy(side).wait_recv()
        make_one_hot(1 + side)
    interior(backward_col)

    for side in range(2):
        weighted_copy(side).wait_recv()
    inject(1, lon - HALO, 0, HALO)
    inject(2, 0, HALO + lon, HALO)

    def backward_diagonal(d, carry):
        diagonal(backward_col, d - 1)
        return carry

    lax.fori_loop(1, HALO + 1, backward_diagonal, 0)

    for k in range(probe_count):
        for i in range(lon):
            for t in range(tiles):
                surface[k * lon + i : k * lon + i + 1, t * LANES : (t + 1) * LANES] = (
                    adj[STEPS][HALO + i, t, k * LEV : k * LEV + 1, :]
                )
    pulled_low = permuted([surface[...]], to_outer)

    def lowest(ref, base):
        return jnp.concatenate([ref[t, base : base + lon, :] for t in range(tiles)], axis=1)

    low = jnp.concatenate(
        [
            lowest(probes_v, k * per_probe)
            + lowest(prior_v, 0) * pulled_low[k * lon : (k + 1) * lon]
            for k in range(probe_count)
        ],
        axis=0,
    )
    height = probe_count * lon
    split_low = jnp.concatenate(split_bf16(low), axis=0)
    own_lon = lax.broadcasted_iota(jnp.int32, (height, LANES), 0) & (lon - 1)
    total_low = jnp.zeros((height, LANES), jnp.float32)
    for i in range(lon):
        out = jnp.dot(split_low, basis_split[i], preferred_element_type=jnp.float32)
        part = out[:height, :LANES] + (out[:height, LANES:] + out[height:, :LANES])
        total_low = total_low + jnp.where(own_lon == i, part, 0.0)
    proj[...] = jnp.zeros_like(proj)
    for k in range(probe_count):
        proj[k : k + 1, :] = jnp.sum(total_low[k * lon : (k + 1) * lon], axis=0, keepdims=True)

    stores = [
        pltpu.make_async_copy(
            hess_v.at[t], hess_out.at[:, pl.ds(t * LANES, LANES)], load_sem.at[4, t]
        )
        for t in range(tiles)
    ]

    def proj_copy(target, source_id):
        return pltpu.make_async_remote_copy(
            src_ref=proj, dst_ref=proj_recv.at[source_id],
            send_sem=proj_ssem.at[target], recv_sem=proj_rsem.at[source_id],
            device_id=(group, target), device_id_type=MESH,
        )

    def send_proj(i, carry):
        proj_copy(lax.rem(me + i, n), me).start()
        return carry

    lax.fori_loop(1, n, send_proj, 0)
    proj_recv[me] = proj[...]

    def finish_pair(d, carry):
        pair = (d, lon - 1 - d)
        pulled = permuted(
            [
                jnp.concatenate([adj[STEPS][HALO + i, t] for t in range(tiles)], axis=1)
                for i in pair
            ],
            to_outer,
        )
        for at, i in enumerate(pair):
            scale = column(prior_v, 0, i)
            for k in range(probe_count):
                value = (
                    column(probes_v, k * per_probe, i)
                    + scale * pulled[at * rows + k * LEV : at * rows + (k + 1) * LEV]
                )
                for t in range(tiles):
                    hess_v[t, pl.ds(k * per_probe + i, LEV, stride=lon), :] = tile(value, t)
        return carry

    lax.fori_loop(0, HALO, finish_pair, 0)
    for store in stores:
        store.start()

    mis_recv[me] = mis_send[me]

    def mis_arrival(i, carry):
        source = lax.rem(me + i, n)
        mis_copy(source, source).wait_recv()
        return carry

    lax.fori_loop(1, n, mis_arrival, 0)

    def store_mis(i, carry):
        misfit_out[pl.ds(i, 1), :] = mis_recv[i]
        return carry

    lax.fori_loop(0, n, store_mis, 0)

    for store in stores:
        store.wait()
    for copy in sends:
        copy.wait_send()

    def finish(i, carry):
        target = lax.rem(me + i, n)
        row_copy(target, me).wait_send()
        mis_copy(target, me).wait_send()
        return carry

    lax.fori_loop(1, n, finish, 0)

    def proj_arrival(i, carry):
        source = lax.rem(me + i, n)
        proj_copy(source, source).wait_recv()
        proj_copy(source, me).wait_send()
        return carry

    lax.fori_loop(1, n, proj_arrival, 0)
    summed = lax.fori_loop(
        1, n, lambda i, acc: acc + proj_recv[i], proj_recv[0]
    )
    values = eigen_values[...]
    coeffs_out[...] = values / (1.0 + values) * summed[0:probe_count]


def finish_kernel(hess, misfit, coeffs, hess_out, misfit_out, coeffs_out):
    hess_out[...] = hess[...]
    misfit_out[...] = misfit[...]
    coeffs_out[...] = coeffs[...]


def local(
    probes, wind_field, prior_scale, eigen_basis, eigen_values, kernel_rows, obs_weight, tile_column
):
    probe_count, _, lon, lat = probes.shape
    rank = eigen_values.shape[0]
    n = kernel_rows.shape[0]
    rows = probe_count * LEV
    ext = lon + 2 * HALO
    total = n * CAP
    tiles = lat // LANES
    f32 = jnp.float32
    vmem = pl.BlockSpec(memory_space=pltpu.VMEM)
    anywhere = pl.BlockSpec(memory_space=pl.ANY)
    dma = pltpu.SemaphoreType.DMA
    hess, misfit, coeffs = pl.pallas_call(
        kernel,
        out_shape=(
            jax.ShapeDtypeStruct((rows * lon, lat), f32),
            jax.ShapeDtypeStruct((n, probe_count * CAP), f32),
            jax.ShapeDtypeStruct((probe_count, rank), f32),
        ),
        in_specs=[anywhere] * 4 + [vmem] * 4,
        out_specs=(anywhere, vmem, vmem),
        scratch_shapes=[
            pltpu.VMEM((tiles, rows * lon, LANES), f32),
            pltpu.VMEM((tiles, 3 * LEV * lon, LANES), f32),
            pltpu.VMEM((tiles, LEV * lon, LANES), f32),
            pltpu.VMEM((lon, lat, rank), f32),
            pltpu.VMEM((lon, lat, 2 * rank), jnp.bfloat16),
            pltpu.VMEM((tiles, rows * lon, LANES), f32),
            pltpu.VMEM((lat, lat), jnp.bfloat16),
            pltpu.VMEM((lat, lat), jnp.bfloat16),
            pltpu.VMEM((probe_count * lon, lat), f32),
            (pltpu.VMEM((ext, tiles, rows, LANES), f32),) * (STEPS + 1),
            (pltpu.VMEM((ext, tiles, rows, LANES), f32),) * (STEPS + 1),
            pltpu.VMEM((ext, tiles, 3, LEV, LANES), f32),
            pltpu.VMEM((n, 1, LEV * CAP + LANES), f32),
            pltpu.VMEM((n, 1, LEV * CAP + LANES), f32),
            pltpu.VMEM((n, LEV * CAP + LANES), f32),
            pltpu.VMEM((3, LEV + 8, total), f32),
            pltpu.VMEM((3, 8, total), f32),
            pltpu.VMEM((3, lat, total), jnp.bfloat16),
            pltpu.VMEM((rows, total), f32),
            pltpu.VMEM((n, LANES), f32),
            pltpu.VMEM((n, 1, LANES), f32),
            pltpu.VMEM((n, 1, LANES), f32),
            pltpu.VMEM((8, rank), f32),
            pltpu.VMEM((n, 8, rank), f32),
            dma((5, tiles)),
            dma((2, 2, HALO)),
            dma((2, 2, HALO)),
            dma((n,)),
            dma((n,)),
            dma((2,)),
            dma((2,)),
            dma((2,)),
            dma((2,)),
            dma((n,)),
            dma((n,)),
            dma((n,)),
            dma((n,)),
            dma((2, HALO, lax.axis_size("groups"))),
            dma((2, HALO, lax.axis_size("groups"))),
        ],
        compiler_params=pltpu.CompilerParams(
            collective_id=1, has_side_effects=True, vmem_limit_bytes=56 * 1024 * 1024
        ),
    )(
        probes.reshape(rows * lon, lat),
        wind_field.reshape(3 * LEV * lon, lat),
        prior_scale.reshape(LEV * lon, lat),
        eigen_basis,
        eigen_values.reshape(1, rank),
        kernel_rows,
        obs_weight,
        tile_column,
    )
    hess, misfit, coeffs = pl.pallas_call(
        finish_kernel,
        out_shape=tuple(jax.ShapeDtypeStruct(x.shape, f32) for x in (hess, misfit, coeffs)),
        in_specs=[vmem] * 3,
        out_specs=(vmem,) * 3,
    )(hess, misfit, coeffs)
    return hess.reshape(probes.shape), misfit, coeffs


def solution(mesh):
    in_specs = (
        P("groups", None, "cells", None),
        P(None, None, "cells", None),
        P(None, "cells", None),
        P("cells", None, None),
        P(),
        P(("groups", "cells"), None),
        P(("groups", "cells"), None),
        P(("groups", "cells"), None),
    )
    out_specs = (P("groups", None, "cells", None), P(("groups", "cells"), None), P("groups", None))
    return jax.shard_map(local, mesh=mesh, in_specs=in_specs, out_specs=out_specs, check_vma=False)
```
